32 devices in a mesh: tok: 8 (over z, y), wid: 4 (over x, core).
Axes of the slice: x: 2, y: 2, z: 4, core: 2. Of those that a mesh axis runs over, the one named last changes fastest.
Arguments:
- queries: bfloat16 [1024, 8192], P('tok', 'wid'), may hold values from -6 to 6
- key_branch: bfloat16 [1024, 8192], P('tok', 'wid'), may hold values from -6 to 6
- value_branch: bfloat16 [1024, 8192], P('tok', 'wid'), may hold values from -6 to 6
- filters: float32 [512, 128], P('wid'), may hold values from -0.5 to 0.5
- out_weight: bfloat16 [8192, 8192], P(None, 'wid'), may hold values from -0.09375 to 0.09375
- cotangent: bfloat16 [1024, 8192], P('tok', 'wid'), may hold values from -6 to 6
Outputs:
- layer_out: bfloat16 [1024, 8192], P('tok', 'wid')
- grad_queries: bfloat16 [1024, 8192], P('tok', 'wid')
- grad_keys: bfloat16 [1024, 8192], P('tok', 'wid')
- grad_values: bfloat16 [1024, 8192], P('tok', 'wid')
- grad_filters: float32 [512, 128], P('wid')
The draws below stay inside these ranges and needn't reach their ends.
All inputs are finite; a program needn't handle non-finite values.
Results may differ from the reference program's by a relative error of at most 0.02.
Values may be sent and summed in bfloat16 or wider, within the bound.
A program may use at most 192 MiB of HBM per device.

```python
import math
import jax
import jax.numpy as jnp
from jax import lax

D = 8192
KERNEL = 128
GROUP = 16
TOKENS = 1024
FILTERS = 512
N_WID = 4


def with_spikes(array, stream_key, source, target, shards_of, factor):
    def block_of(position):
        return (jnp.arange(array.shape[position]) // (array.shape[position] // shards_of)).reshape((-1,) + (1,) * (array.ndim - 1 - position))

    one_side = jax.random.permutation(stream_key, shards_of)[block_of(target)]
    second = (block_of(target) + shards_of // 2) % shards_of
    return jnp.where((block_of(source) == one_side) | (block_of(source) == second), factor * array, array)


def level_of(key, shape, pieces, low, high):
    gain, own = 1.0, jax.random.fold_in(key, 6)
    for dim, blocks in pieces:
        heights = jnp.exp(jax.random.uniform(jax.random.fold_in(own, dim), (blocks,), jnp.float32, low / len(pieces), high / len(pieces)))
        gain = gain * jnp.repeat(heights, shape[dim] // blocks).reshape([-1 if axis == dim else 1 for axis in range(len(shape))])
    return gain


def bell_draw(rng, shape, scale, reach, pieces=(), held_as=jnp.bfloat16):
    result = scale * jax.random.normal(rng, shape, jnp.float32)
    if pieces:
        result = result * level_of(rng, shape, pieces, -0.22, 0.18)
    return jnp.clip(result, -reach, reach).astype(held_as)


def noise_with(rng, shape, scale, limit, shards, heavy, kind=jnp.bfloat16):
    values = scale * jax.random.normal(rng, shape, jnp.float32)
    if shards:
        values = values * level_of(rng, shape, shards, -0.22, 0.18)
    return jnp.clip(with_spikes(values, jax.random.fold_in(rng, 3), *heavy), -limit, limit).astype(kind)


def setup_inputs(seed: int = 0) -> dict:
    seeds = jax.random.split(jax.random.key(seed), 7)
    return {
        "queries": bell_draw(seeds[0], (TOKENS, D), 1.0, 6.0, ((0, 8), (1, 4))),
        "key_branch": bell_draw(seeds[1], (TOKENS, D), 1.0, 6.0, ((0, 8), (1, 4))),
        "value_branch": bell_draw(seeds[2], (TOKENS, D), 1.0, 6.0, ((0, 8), (1, 4))),
        "filters": bell_draw(seeds[3], (FILTERS, KERNEL), KERNEL ** -0.5, 0.5, ((0, 4),), jnp.float32),
        "out_weight": noise_with(seeds[4], (D, D), D ** -0.5, 0.09375, ((1, 4),), (1, 0, 4, 2.0)),
        "cotangent": bell_draw(seeds[5], (TOKENS, D), 1.0, 6.0, ((0, 8), (1, 4))),
    }


def reference(queries, key_branch, value_branch, filters, out_weight, cotangent):
    kv = (key_branch.astype(jnp.float32) * value_branch.astype(jnp.float32)).astype(jnp.bfloat16)
    kv_float = kv.astype(jnp.float32)
    chan_filters = jnp.repeat(filters, GROUP, axis=0)
    padded = jnp.concatenate([jnp.zeros((KERNEL, D), jnp.float32), kv_float], axis=0)

    def conv_tap(j, total):
        start = (KERNEL - j).astype(jnp.int32)
        shifted = lax.dynamic_slice_in_dim(padded, start, TOKENS, 0)
        taps = lax.dynamic_index_in_dim(chan_filters, j.astype(jnp.int32), 1, keepdims=False)
        return total + shifted * taps
    conv = lax.fori_loop(0, KERNEL, conv_tap, jnp.zeros((TOKENS, D), jnp.float32))
    gated = (queries.astype(jnp.float32) * conv).astype(jnp.bfloat16)
    layer_out = jnp.dot(gated, out_weight, preferred_element_type=jnp.float32).astype(jnp.bfloat16)
    block_width = D // N_WID

    def grad_block(n, total):
        start = (n * block_width).astype(jnp.int32)
        cot_block = lax.dynamic_slice_in_dim(cotangent, start, block_width, 1)
        weight_block = lax.dynamic_slice_in_dim(out_weight, start, block_width, 1)
        part = lax.dot_general(cot_block, weight_block, (((1,), (1,)), ((), ())), preferred_element_type=jnp.float32)
        rounded = lax.optimization_barrier(part.astype(jnp.bfloat16))
        return total + rounded.astype(jnp.float32)
    grad_gated = lax.fori_loop(0, N_WID, grad_block, jnp.zeros((TOKENS, D), jnp.float32))
    grad_conv = (grad_gated * queries.astype(jnp.float32)).astype(jnp.bfloat16)
    grad_queries = (grad_gated * conv).astype(jnp.bfloat16)
    grad_float = grad_conv.astype(jnp.float32)
    grad_padded = jnp.concatenate([grad_float, jnp.zeros((KERNEL, D), jnp.float32)], axis=0)

    def back_tap(j, total):
        shifted = lax.dynamic_slice_in_dim(grad_padded, j.astype(jnp.int32), TOKENS, 0)
        taps = lax.dynamic_index_in_dim(chan_filters, j.astype(jnp.int32), 1, keepdims=False)
        return total + shifted * taps
    grad_kv = lax.fori_loop(0, KERNEL, back_tap, jnp.zeros((TOKENS, D), jnp.float32))
    grad_keys = (grad_kv * value_branch.astype(jnp.float32)).astype(jnp.bfloat16)
    grad_values = (grad_kv * key_branch.astype(jnp.float32)).astype(jnp.bfloat16)

    def filter_tap(j):
        start = (KERNEL - j).astype(jnp.int32)
        shifted = lax.dynamic_slice_in_dim(padded, start, TOKENS, 0)
        return lax.optimization_barrier(jnp.sum(grad_float * shifted, axis=0))
    per_tap = lax.map(filter_tap, jnp.arange(KERNEL, dtype=jnp.int32))
    grouped = per_tap.T.reshape(FILTERS, GROUP, KERNEL).sum(axis=1)
    grad_filters = grouped * (1.0 / math.sqrt(TOKENS * GROUP))
    return (layer_out, grad_queries, grad_keys, grad_values, grad_filters)
```

```python
import functools
import math

import jax
import jax.numpy as jnp
from jax import lax
from jax.experimental import pallas as pl
from jax.experimental.pallas import tpu as pltpu
from jax.sharding import PartitionSpec as P

bf16, f32 = jnp.bfloat16, jnp.float32


def iota(shape, dim):
    return lax.broadcasted_iota(jnp.int32, shape, dim)


def as_mask(condition):
    return jnp.where(condition, 1.0, 0.0).astype(bf16)


def dot(a, b):
    return jnp.dot(a, b, preferred_element_type=f32)


def fanned(rows):
    return pltpu.roll(rows, 0, 1, stride=1, stride_axis=0)


def conv_tile(filters, own, other, keep, group_size):
    groups, kernel = filters.shape
    data = jnp.concatenate([own, other], axis=1)
    parts = []
    for g in range(groups):
        ring = fanned(jnp.broadcast_to(filters[g : g + 1], (kernel, kernel))).astype(bf16)
        kept = ring * keep
        taps = jnp.concatenate([kept, ring - kept], axis=0)
        parts.append(dot(data[g * group_size : (g + 1) * group_size], taps))
    return jnp.concatenate(parts, axis=0)


def filter_tile(before, own, grads, mirror, groups, group_size):
    tile, kernel = own.shape
    half = kernel // 2
    window = jnp.concatenate([before, own], axis=1)
    later = jnp.concatenate([window[:, half:], window[:, :half]], axis=1)
    data = jnp.concatenate([window, later], axis=0)
    turned = dot(mirror, grads.T).astype(bf16)
    turned = jnp.concatenate([turned[:half], turned[half:]], axis=1)
    owner = lax.rem(iota((half, 2 * tile), 1), tile) // group_size
    now = iota((half, kernel), 0) + iota((half, kernel), 1) <= half - 1
    rows = []
    for g in range(groups):
        part = dot(turned * as_mask(owner == g), data)
        square = jnp.where(now, part[:, kernel:], part[:, :kernel])
        rows.append(jnp.sum(fanned(square), axis=0, keepdims=True))
    return jnp.concatenate(rows, axis=0)


def kernel(
    sizes, scale,
    q_hbm, k_hbm, v_hbm, f_hbm, w_hbm, cot_hbm,
    out_hbm, gq_hbm, gk_hbm, gv_hbm, gf_hbm,
    q_ref, k_ref, v_ref, f_ref, cot_ref, w_buf, cot_t, q_t, kv_t, rim_t, conv_t, part_t,
    sib_out, sib_in, pre_out, pre_in, gather, total, gc_t, gcn_t,
    out_buf, gq_buf, gk_buf, gv_buf, frev_buf, local_buf, terms_buf, all_buf,
    in_sem, out_sem, w_sem, kv_send, kv_recv, sib_send, sib_recv, pre_send, pre_recv,
    own_send, own_recv, peer_send, peer_recv, fwd_send, fwd_recv, gc_send, gc_recv,
    term_send, term_recv, sum_send, sum_recv,
):
    n_tok, n_wid, tile, piece, owners = sizes
    length, width = q_ref.shape
    groups, kernel_size = f_ref.shape
    group_size = width // groups
    tile_groups = tile // group_size
    pieces = width // piece
    tiles = piece // tile
    chips = n_wid // 2
    steps = (chips - 1) * pieces
    rows = groups // owners
    tok, me = lax.axis_index("tok"), lax.axis_index("wid")
    chip, core = me // 2, lax.rem(me, 2)
    sibling = chip * 2 + 1 - core
    other_chips = [lax.rem(chip + off, chips) for off in range(1, chips)]
    other_toks = [lax.rem(tok + off, n_tok) for off in range(1, n_tok)]
    has_next, has_previous = tok < n_tok - 1, tok > 0

    def step_of(i):
        return lax.rem(chip + 1 + i // pieces, chips), lax.rem(i, pieces)

    def span(h):
        return pl.ds(pl.multiple_of(h * piece, piece), piece)

    def tile_of(h, i):
        return pl.ds(pl.multiple_of(h * piece + i * tile, tile), tile)

    def groups_of(h, i):
        return pl.ds(pl.multiple_of((h * tiles + i) * tile_groups, tile_groups), tile_groups)

    ins = [
        pltpu.make_async_copy(src, dst, in_sem.at[i])
        for i, (src, dst) in enumerate(
            [(k_hbm, k_ref), (v_hbm, v_ref), (cot_hbm, cot_ref), (q_hbm, q_ref), (f_hbm, f_ref)]
        )
    ]
    for copy in ins[:3]:
        copy.start()

    def w_rows(block, h):
        return pl.ds(pl.multiple_of(block * width + h * piece, piece), piece)

    def w_copy(block, h):
        at = w_rows(block, h)
        return pltpu.make_async_copy(w_hbm.at[at], w_buf.at[at], w_sem.at[block * pieces + h])

    @pl.loop(0, steps)
    def _(i):
        p, h = step_of(i)
        w_copy(p * 2 + 1 - core, h).start()
        w_copy(p * 2 + core, h).start()

    for copy in ins[3:]:
        copy.start()
    for block in (sibling, me):

        @pl.loop(0, pieces)
        def _(h):
            w_copy(block, h).start()

    def remote(src, dst, send, recv, **where):
        return pltpu.make_async_remote_copy(
            src_ref=src, dst_ref=dst, send_sem=send, recv_sem=recv,
            device_id=where, device_id_type=pl.DeviceIdType.MESH,
        )

    barrier = pltpu.get_barrier_semaphore()
    for where in (
        [{"wid": sibling}] + [{"wid": p * 2 + core} for p in other_chips] + [{"tok": t} for t in other_toks]
    ):
        pl.semaphore_signal(barrier, inc=1, device_id=where, device_id_type=pl.DeviceIdType.MESH)

    ins[0].wait()
    ins[1].wait()

    @pl.loop(0, pieces)
    def _(h):
        for i in range(tiles):
            at = tile_of(h, i)
            kv_t[at, :] = (k_ref[:, at].astype(f32) * v_ref[:, at].astype(f32)).astype(bf16).T

    ins[2].wait()

    @pl.loop(0, pieces)
    def _(h):
        for i in range(tiles):
            at = tile_of(h, i)
            cot_t[at, :] = cot_ref[:, at].T

    pl.semaphore_wait(barrier, 1 + len(other_chips) + len(other_toks))

    def kv_copy(h):
        return remote(
            kv_t.at[span(h)], rim_t.at[span(h)], kv_send.at[h], kv_recv.at[h], tok=lax.rem(tok + 1, n_tok)
        )

    def gc_copy(h):
        return remote(
            gc_t.at[span(h)], gcn_t.at[span(h)], gc_send.at[h], gc_recv.at[h], tok=lax.rem(tok + n_tok - 1, n_tok)
        )

    @pl.when(has_next)
    def _():
        for h in range(pieces):
            kv_copy(h).start()

    def sib_copy(p, h):
        sem = p * pieces + h
        return remote(
            sib_out.at[p, span(h)], sib_in.at[p, span(h)], sib_send.at[sem], sib_recv.at[sem], wid=sibling
        )

    def pre_copy(p, slot, h):
        return remote(
            pre_out.at[p, span(h)], pre_in.at[slot, span(h)],
            pre_send.at[p * pieces + h], pre_recv.at[slot * pieces + h], wid=p * 2 + core,
        )

    def grad_rows(block, h):
        w_copy(block, h).wait()
        return dot(w_buf[w_rows(block, h), :], cot_t[...])

    def send_sum(i):
        p, h = step_of(i)
        sib_copy(p, h).wait_recv()
        pre_out[p, span(h), :] = (part_t[span(h), :] + sib_in[p, span(h), :].astype(f32)).astype(bf16)
        pre_copy(p, chip, h).start()

    @pl.loop(0, steps)
    def _(i):
        p, h = step_of(i)
        sib_out[p, span(h), :] = grad_rows(p * 2 + 1 - core, h).astype(bf16)
        sib_copy(p, h).start()
        pl.when(i > 0)(lambda: send_sum(i - 1))
        part_t[span(h), :] = grad_rows(p * 2 + core, h)

    @pl.loop(0, pieces)
    def _(h):
        sib_out[chip, span(h), :] = grad_rows(sibling, h).astype(bf16)
        sib_copy(chip, h).start()
        pl.when(h == 0)(lambda: send_sum(steps - 1))

    ins[3].wait()
    ins[4].wait()
    lanes, sublanes = iota((kernel_size, kernel_size), 1), iota((kernel_size, kernel_size), 0)
    flip = as_mask(lax.rem(lanes + sublanes, kernel_size) == 0)
    frev_buf[...] = dot(f_ref[...].astype(bf16), flip)

    def own_copy(h, slot):
        return remote(
            gather.at[me, :, span(h)], gather.at[slot, :, span(h)], own_send.at[h], own_recv.at[h], wid=sibling
        )

    def peer_copy(p, h, slot, slot_chip):
        return remote(
            gather.at[me, :, span(h)], gather.at[slot, :, span(h)],
            peer_send.at[p * pieces + h], peer_recv.at[slot_chip * pieces + h], wid=p * 2 + core,
        )

    def fwd_copy(p, h, slot):
        return remote(
            gather.at[p * 2 + core, :, span(h)], gather.at[slot, :, span(h)],
            fwd_send.at[p * pieces + h], fwd_recv.at[p * pieces + h], wid=sibling,
        )

    @pl.when(jnp.logical_not(has_previous))
    def _():
        rim_t[...] = jnp.zeros_like(rim_t)

    def forward_piece(h):
        @pl.when(has_previous)
        def _():
            kv_copy(h).wait_recv()

        keep = as_mask(sublanes <= lanes)
        for i in range(tiles):
            at = tile_of(h, i)
            turned = q_ref[:, at].T
            conv = conv_tile(f_ref[groups_of(h, i), :], kv_t[at, :], rim_t[at, :], keep, group_size)
            q_t[at, :] = turned
            conv_t[at, :] = conv
            gather[me, :, at] = (turned.astype(f32) * conv).astype(bf16).T
        for p in other_chips:
            peer_copy(p, h, me, chip).start()
        own_copy(h, me).start()

    @pl.loop(0, pieces)
    def _(h):
        forward_piece(h)
        part_t[span(h), :] = grad_rows(me, h)

    mirror = as_mask(
        jnp.logical_and(
            lanes // (kernel_size // 2) == sublanes // (kernel_size // 2),
            lax.rem(lanes, kernel_size // 2) + lax.rem(sublanes, kernel_size // 2) == kernel_size // 2 - 1,
        )
    )

    @pl.loop(0, pieces)
    def _(h):
        sib_copy(chip, h).wait_recv()
        for p in other_chips:
            pre_copy(p, p, h).wait_recv()
        for i in range(tiles):
            at = tile_of(h, i)
            grad_gated = part_t[at, :] + sib_in[chip, at, :].astype(f32)
            for p in other_chips:
                grad_gated = grad_gated + pre_in[p, at, :].astype(f32)
            gc_t[at, :] = (grad_gated * q_t[at, :].astype(f32)).astype(bf16)
            gq_buf[:, at] = (grad_gated * conv_t[at, :]).astype(bf16).T

        @pl.when(has_previous)
        def _():
            gc_copy(h).start()

        for i in range(tiles):
            at = tile_of(h, i)
            local_buf[groups_of(h, i), :] = filter_tile(
                rim_t[at, :], kv_t[at, :], gc_t[at, :], mirror, tile_groups, group_size
            )

    outs = [
        pltpu.make_async_copy(src, dst, out_sem.at[i])
        for i, (src, dst) in enumerate(
            [(gq_buf, gq_hbm), (gk_buf, gk_hbm), (gv_buf, gv_hbm), (out_buf, out_hbm), (all_buf, gf_hbm)]
        )
    ]
    outs[0].start()
    back = jnp.where(
        lax.rem(lanes + sublanes + kernel_size // 2 + 1, kernel_size) == 0, 1.0, 0.0
    ).astype(f32)
    local_buf[...] = jnp.dot(local_buf[...], back, preferred_element_type=f32, precision=lax.Precision.HIGHEST)

    def owned(t):
        return pl.ds(pl.multiple_of(t * rows, rows), rows)

    def term_copy(t, slot):
        return remote(local_buf.at[owned(lax.rem(t, owners))], terms_buf.at[slot], term_send.at[t], term_recv.at[slot], tok=t)

    def sum_copy(t, owner):
        return remote(all_buf.at[owned(owner)], all_buf.at[owned(owner)], sum_send.at[t], sum_recv.at[owner], tok=t)

    def if_owner(t, action):
        if owners == n_tok:
            action()
        else:
            pl.when(t < owners)(action)

    for t in other_toks:
        if_owner(t, lambda t=t: term_copy(t, tok).start())

    def project(block, start, depth, first=False):
        deep = pl.ds(pl.multiple_of(block * width + start, depth), depth)
        product = dot(gather[block, :, pl.ds(pl.multiple_of(start, depth), depth)], w_buf[deep, :])
        total[...] = product if first else total[...] + product

    project(me, 0, width, True)
    for h in range(pieces):
        own_copy(h, sibling).wait_recv()
    project(sibling, 0, width)

    def sum_terms():
        for t in other_toks:
            term_copy(t, t).wait_recv()
        terms_buf[tok] = local_buf[owned(tok), :]
        all_buf[owned(tok), :] = jnp.sum(terms_buf[...], axis=0) * scale
        for t in other_toks:
            sum_copy(t, tok).start()

    if_owner(tok, sum_terms)

    @pl.when(jnp.logical_not(has_next))
    def _():
        gcn_t[...] = jnp.zeros_like(gcn_t)

    @pl.loop(0, pieces)
    def _(h):
        @pl.when(has_next)
        def _():
            gc_copy(h).wait_recv()

        keep = as_mask(lanes <= sublanes)
        for i in range(tiles):
            at = tile_of(h, i)
            grad_kv = conv_tile(frev_buf[groups_of(h, i), :], gc_t[at, :], gcn_t[at, :], keep, group_size).T
            gk_buf[:, at] = (grad_kv * v_ref[:, at].astype(f32)).astype(bf16)
            gv_buf[:, at] = (grad_kv * k_ref[:, at].astype(f32)).astype(bf16)

    outs[1].start()
    outs[2].start()

    def last_half(i):
        p, h = step_of(i)
        fwd_copy(p, h, p * 2 + 1 - core).wait_recv()
        project(p * 2 + 1 - core, h * piece, piece)

    @pl.loop(0, steps)
    def _(i):
        p, h = step_of(i)
        peer_copy(p, h, p * 2 + core, p).wait_recv()
        fwd_copy(p, h, p * 2 + core).start()
        pl.when(i > 0)(lambda: last_half(i - 1))
        project(p * 2 + core, h * piece, piece)

    last_half(steps - 1)
    out_buf[...] = total[...].astype(bf16)
    outs[3].start()
    for t in other_toks:
        if_owner(t, lambda t=t: sum_copy(t, t).wait_recv())
    outs[4].start()

    for h in range(pieces):
        pl.when(has_next)(lambda h=h: kv_copy(h).wait_send())
        pl.when(has_previous)(lambda h=h: gc_copy(h).wait_send())
        sib_copy(chip, h).wait_send()
        own_copy(h, me).wait_send()

    @pl.loop(0, steps)
    def _(i):
        p, h = step_of(i)
        sib_copy(p, h).wait_send()
        pre_copy(p, chip, h).wait_send()
        peer_copy(p, h, me, chip).wait_send()
        fwd_copy(p, h, p * 2 + core).wait_send()

    for t in other_toks:
        if_owner(t, lambda t=t: term_copy(t, tok).wait_send())

    def sums_sent():
        for t in other_toks:
            sum_copy(t, tok).wait_send()

    if_owner(tok, sums_sent)
    for copy in outs:
        copy.wait()


def hand_on(*refs):
    count = len(refs) // 2
    sems = refs[-1]
    copies = [pltpu.make_async_copy(refs[i], refs[count + i], sems.at[i]) for i in range(count)]
    for copy in copies:
        copy.start()
    for copy in copies:
        copy.wait()


def local(queries, key_branch, value_branch, filters, out_weight, cotangent):
    length, width = queries.shape
    groups, kernel_size = filters.shape
    n_tok, n_wid = lax.axis_size("tok"), lax.axis_size("wid")
    chips = n_wid // 2
    group_size = width // groups
    tile = min(128, width // 2)
    piece = max(tile, width // 4)
    pieces = width // piece
    owners = min(n_tok, groups // 8)
    wide = jax.ShapeDtypeStruct((length, width), bf16)
    results = [wide] * 4 + [jax.ShapeDtypeStruct(filters.shape, f32)]
    dma = pltpu.SemaphoreType.DMA
    hbm = pl.BlockSpec(memory_space=pl.ANY)
    flat, turned = pltpu.VMEM((length, width), bf16), pltpu.VMEM((width, length), bf16)
    turned_f32 = pltpu.VMEM((width, length), f32)
    by_chip = pltpu.VMEM((chips, width, length), bf16)
    taps = pltpu.VMEM(filters.shape, f32)
    scale = 1.0 / math.sqrt(length * n_tok * group_size)
    outs = pl.pallas_call(
        functools.partial(kernel, (n_tok, n_wid, tile, piece, owners), scale),
        in_specs=[hbm] * 6,
        out_specs=[hbm] * 5,
        out_shape=results,
        scratch_shapes=[
            flat, flat, flat, taps, flat,
            pltpu.VMEM(out_weight.shape, bf16),
            turned, turned, turned, turned, turned_f32, turned_f32,
            by_chip, by_chip, by_chip, by_chip,
            pltpu.VMEM((n_wid, length, width), bf16),
            pltpu.VMEM((length, width), f32),
            turned, turned,
            flat, flat, flat, flat,
            taps, taps,
            pltpu.VMEM((n_tok, groups // owners, kernel_size), f32),
            taps,
            dma((5,)), dma((5,)), dma((n_wid * pieces,)),
            dma((pieces,)), dma((pieces,)),
            dma((chips * pieces,)), dma((chips * pieces,)), dma((chips * pieces,)), dma((chips * pieces,)),
            dma((pieces,)), dma((pieces,)),
            dma((chips * pieces,)), dma((chips * pieces,)), dma((chips * pieces,)), dma((chips * pieces,)),
            dma((pieces,)), dma((pieces,)),
            dma((n_tok,)), dma((n_tok,)), dma((n_tok,)), dma((n_tok,)),
        ],
        compiler_params=pltpu.CompilerParams(
            collective_id=0, has_side_effects=True, vmem_limit_bytes=60 * 2**20
        ),
        cost_estimate=pl.CostEstimate(
            flops=4 * length * width * width * n_wid, bytes_accessed=2 * width * width * n_wid, transcendentals=0
        ),
    )(queries, key_branch, value_branch, filters, out_weight, cotangent)
    return pl.pallas_call(
        hand_on, in_specs=[hbm] * 5, out_specs=[hbm] * 5, out_shape=results, scratch_shapes=[dma((5,))]
    )(*outs)


def solution(mesh):
    return jax.shard_map(
        local,
        mesh=mesh,
        in_specs=(
            P("tok", "wid"),
            P("tok", "wid"),
            P("tok", "wid"),
            P("wid", None),
            P(None, "wid"),
            P("tok", "wid"),
        ),
        out_specs=(
            P("tok", "wid"),
            P("tok", "wid"),
            P("tok", "wid"),
            P("tok", "wid"),
            P("wid", None),
        ),
        check_vma=False,
    )
```

```python
import functools
import math

import jax
import jax.numpy as jnp
from jax import lax
from jax.experimental import pallas as pl
from jax.experimental.pallas import tpu as pltpu
from jax.sharding import PartitionSpec as P

bf16, f32 = jnp.bfloat16, jnp.float32


def iota(shape, dim):
    return lax.broadcasted_iota(jnp.int32, shape, dim)


def as_mask(condition):
    return jnp.where(condition, 1.0, 0.0).astype(bf16)


def dot(a, b):
    return jnp.dot(a, b, preferred_element_type=f32)


def fanned(rows):
    return pltpu.roll(rows, 0, 1, stride=1, stride_axis=0)


def conv_tile(filters, own, other, keep, group_size):
    groups, kernel = filters.shape
    data = jnp.concatenate([own, other], axis=1)
    parts = []
    for g in range(groups):
        ring = fanned(jnp.broadcast_to(filters[g : g + 1], (kernel, kernel))).astype(bf16)
        kept = ring * keep
        taps = jnp.concatenate([kept, ring - kept], axis=0)
        parts.append(dot(data[g * group_size : (g + 1) * group_size], taps))
    return jnp.concatenate(parts, axis=0)


def filter_tile(before, own, turned, groups, group_size):
    tile, kernel = own.shape
    half = kernel // 2
    window = jnp.concatenate([before, own], axis=1)
    later = jnp.concatenate([window[:, half:], window[:, :half]], axis=1)
    data = jnp.concatenate([window, later], axis=0)
    turned = jnp.concatenate([turned[:half], turned[half:]], axis=1)
    owner = lax.rem(iota((half, 2 * tile), 1), tile) // group_size
    parts = dot(jnp.concatenate([turned * as_mask(owner == g) for g in range(groups)], axis=0), data)
    now = iota((half, kernel), 0) + iota((half, kernel), 1) <= half - 1
    rows = []
    for g in range(groups):
        part = parts[g * half : (g + 1) * half]
        square = jnp.where(now, part[:, kernel:], part[:, :kernel])
        rows.append(jnp.sum(fanned(square), axis=0, keepdims=True))
    return jnp.concatenate(rows, axis=0)


def each(count, body):
    if count <= 4:
        for i in range(count):
            body(i)
    else:
        pl.loop(0, count)(body)


def when(condition, action):
    if isinstance(condition, bool):
        if condition:
            action()
    else:
        pl.when(condition)(action)


def kernel(
    sizes, scale,
    q_hbm, k_hbm, v_hbm, f_hbm, w_hbm, cot_hbm,
    out_hbm, gq_hbm, gk_hbm, gv_hbm, gf_hbm,
    q_ref, k_ref, v_ref, f_ref, cot_ref, w_buf, cot_t, q_t, kv_t, rim_t, conv_t, part_t,
    sib_out, sib_in, pre_out, pre_in, gather, total, gc_t, gcn_t,
    out_buf, gq_buf, gk_buf, gv_buf, frev_buf, local_buf, terms_buf, all_buf,
    in_sem, out_sem, w_sem, kv_send, kv_recv, sib_send, sib_recv, pre_send, pre_recv,
    own_send, own_recv, peer_send, peer_recv, fwd_send, fwd_recv, gc_send, gc_recv,
    term_send, term_recv, sum_send, sum_recv,
):
    n_tok, n_wid, tile, piece, owners = sizes
    length, width = q_ref.shape
    groups, kernel_size = f_ref.shape
    group_size = width // groups
    tile_groups = tile // group_size
    pieces = width // piece
    tiles = piece // tile
    chips = n_wid // 2
    steps = (chips - 1) * pieces
    rows = groups // owners
    tok, me = lax.axis_index("tok"), lax.axis_index("wid")
    chip, core = me // 2, lax.rem(me, 2)
    sibling = chip * 2 + 1 - core
    other_chips = [lax.rem(chip + off, chips) for off in range(1, chips)]
    other_toks = [lax.rem(tok + off, n_tok) for off in range(1, n_tok)]
    has_next, has_previous = tok < n_tok - 1, tok > 0

    def step_of(i):
        return lax.rem(chip + 1 + i // pieces, chips), lax.rem(i, pieces)

    def span(h):
        return pl.ds(pl.multiple_of(h * piece, piece), piece)

    def tile_of(h, i):
        return pl.ds(pl.multiple_of(h * piece + i * tile, tile), tile)

    def groups_of(h, i):
        return pl.ds(pl.multiple_of((h * tiles + i) * tile_groups, tile_groups), tile_groups)

    ins = [
        pltpu.make_async_copy(src, dst, in_sem.at[i])
        for i, (src, dst) in enumerate(
            [(k_hbm, k_ref), (v_hbm, v_ref), (cot_hbm, cot_ref), (q_hbm, q_ref), (f_hbm, f_ref)]
        )
    ]
    for copy in ins[:3]:
        copy.start()

    def w_rows(block, h):
        return pl.ds(pl.multiple_of(block * width + h * piece, piece), piece)

    def w_copy(block, h):
        at = w_rows(block, h)
        return pltpu.make_async_copy(w_hbm.at[at], w_buf.at[at], w_sem.at[block * pieces + h])

    @pl.loop(0, steps)
    def _(i):
        p, h = step_of(i)
        w_copy(p * 2 + 1 - core, h).start()
        w_copy(p * 2 + core, h).start()

    for copy in ins[3:]:
        copy.start()
    for block in (sibling, me):

        @pl.loop(0, pieces)
        def _(h):
            w_copy(block, h).start()

    def remote(src, dst, send, recv, **where):
        return pltpu.make_async_remote_copy(
            src_ref=src, dst_ref=dst, send_sem=send, recv_sem=recv,
            device_id=where, device_id_type=pl.DeviceIdType.MESH,
        )

    barrier = pltpu.get_barrier_semaphore()
    for where in (
        [{"wid": sibling}] + [{"wid": p * 2 + core} for p in other_chips] + [{"tok": t} for t in other_toks]
    ):
        pl.semaphore_signal(barrier, inc=1, device_id=where, device_id_type=pl.DeviceIdType.MESH)

    ins[0].wait()
    ins[1].wait()

    @pl.loop(0, pieces)
    def _(h):
        for i in range(tiles):
            at = tile_of(h, i)
            kv_t[at, :] = (k_ref[:, at].astype(f32) * v_ref[:, at].astype(f32)).astype(bf16).T

    ins[2].wait()

    @pl.loop(0, pieces)
    def _(h):
        for i in range(tiles):
            at = tile_of(h, i)
            cot_t[at, :] = cot_ref[:, at].T

    def kv_copy(h):
        return remote(
            kv_t.at[span(h)], rim_t.at[span(h)], kv_send.at[h], kv_recv.at[h], tok=lax.rem(tok + 1, n_tok)
        )

    def gc_copy(h):
        return remote(
            gc_t.at[span(h)], gcn_t.at[span(h)], gc_send.at[h], gc_recv.at[h], tok=lax.rem(tok + n_tok - 1, n_tok)
        )

    def sib_copy(p, h):
        sem = p * pieces + h
        return remote(
            sib_out.at[p, span(h)], sib_in.at[p, span(h)], sib_send.at[sem], sib_recv.at[sem], wid=sibling
        )

    def pre_copy(p, slot, h):
        return remote(
            pre_out.at[p, span(h)], pre_in.at[slot, span(h)],
            pre_send.at[p * pieces + h], pre_recv.at[slot * pieces + h], wid=p * 2 + core,
        )

    def send_sum(i):
        p, h = step_of(i)
        sib_copy(p, h).wait_recv()
        pre_out[p, span(h), :] = (part_t[span(h), :] + sib_in[p, span(h), :].astype(f32)).astype(bf16)
        pre_copy(p, chip, h).start()

    def two_parts(i):
        p, h = step_of(i)
        w_copy(p * 2 + 1 - core, h).wait()
        w_copy(p * 2 + core, h).wait()
        sib_out[p, span(h), :] = dot(w_buf[w_rows(p * 2 + 1 - core, h), :], cot_t[...]).astype(bf16)
        part_t[span(h), :] = dot(w_buf[w_rows(p * 2 + core, h), :], cot_t[...])

    def own_parts(block, store):
        for h in range(pieces):
            w_copy(block, h).wait()
        size = 2 * piece if pieces % 2 == 0 else piece
        for start in range(0, width, size):
            rows_at = pl.ds(pl.multiple_of(block * width + start, size), size)
            store(pl.ds(start, size), dot(w_buf[rows_at, :], cot_t[...]))

    two_parts(0)
    pl.semaphore_wait(barrier, 1 + len(other_chips) + len(other_toks))
    sib_copy(*step_of(0)).start()

    @pl.when(has_next)
    def _():
        for h in range(pieces):
            kv_copy(h).start()

    def sum_step(j):
        i = j + 1
        if pieces > 1:
            two_parts(i)
            sib_copy(*step_of(i)).start()
            send_sum(i - 1)
        else:
            send_sum(i - 1)
            two_parts(i)
            sib_copy(*step_of(i)).start()

    each(steps - 1, sum_step)

    def store_sibling(at, product):
        sib_out[chip, at, :] = product.astype(bf16)

    own_parts(sibling, store_sibling)
    for h in range(pieces):
        sib_copy(chip, h).start()
    send_sum(steps - 1)

    ins[3].wait()
    ins[4].wait()
    lanes, sublanes = iota((kernel_size, kernel_size), 1), iota((kernel_size, kernel_size), 0)
    flip = as_mask(lax.rem(lanes + sublanes, kernel_size) == 0)
    frev_buf[...] = dot(f_ref[...].astype(bf16), flip)

    def own_copy(h, slot):
        return remote(
            gather.at[me, :, span(h)], gather.at[slot, :, span(h)], own_send.at[h], own_recv.at[h], wid=sibling
        )

    def peer_copy(p, h, slot, slot_chip):
        return remote(
            gather.at[me, :, span(h)], gather.at[slot, :, span(h)],
            peer_send.at[p * pieces + h], peer_recv.at[slot_chip * pieces + h], wid=p * 2 + core,
        )

    def fwd_copy(p, h, slot):
        return remote(
            gather.at[p * 2 + core, :, span(h)], gather.at[slot, :, span(h)],
            fwd_send.at[p * pieces + h], fwd_recv.at[p * pieces + h], wid=sibling,
        )

    @pl.when(jnp.logical_not(has_previous))
    def _():
        rim_t[...] = jnp.zeros_like(rim_t)

    def forward_piece(h):
        @pl.when(has_previous)
        def _():
            kv_copy(h).wait_recv()

        keep = as_mask(sublanes <= lanes)
        for i in range(tiles):
            at = tile_of(h, i)
            turned = q_ref[:, at].T
            conv = conv_tile(f_ref[groups_of(h, i), :], kv_t[at, :], rim_t[at, :], keep, group_size)
            q_t[at, :] = turned
            conv_t[at, :] = conv
            gather[me, :, at] = (turned.astype(f32) * conv).astype(bf16).T
        for p in other_chips:
            peer_copy(p, h, me, chip).start()
        own_copy(h, me).start()

    def store_own(at, product):
        part_t[at, :] = product

    forward_piece(0)
    own_parts(me, store_own)
    for h in range(1, pieces - 1):
        forward_piece(h)

    mirror = as_mask(
        jnp.logical_and(
            lanes // (kernel_size // 2) == sublanes // (kernel_size // 2),
            lax.rem(lanes, kernel_size // 2) + lax.rem(sublanes, kernel_size // 2) == kernel_size // 2 - 1,
        )
    )

    def backward_piece(h):
        sib_copy(chip, h).wait_recv()
        for p in other_chips:
            pre_copy(p, p, h).wait_recv()
        turned = []
        for i in range(tiles):
            at = tile_of(h, i)
            grad_gated = part_t[at, :] + sib_in[chip, at, :].astype(f32)
            for p in other_chips:
                grad_gated = grad_gated + pre_in[p, at, :].astype(f32)
            grad_conv = (grad_gated * q_t[at, :].astype(f32)).astype(bf16)
            gc_t[at, :] = grad_conv
            turned.append(grad_conv.T)
            gq_buf[:, at] = (grad_gated * conv_t[at, :]).astype(bf16).T

        @pl.when(has_previous)
        def _():
            gc_copy(h).start()

        turned = dot(mirror, jnp.concatenate(turned, axis=1)).astype(bf16)
        for i in range(tiles):
            at = tile_of(h, i)
            local_buf[groups_of(h, i), :] = filter_tile(
                rim_t[at, :], kv_t[at, :], turned[:, i * tile : (i + 1) * tile], tile_groups, group_size
            )

    for h in range(pieces):
        if h == pieces // 2 and pieces > 1:
            forward_piece(pieces - 1)
        backward_piece(h)

    outs = [
        pltpu.make_async_copy(src, dst, out_sem.at[i])
        for i, (src, dst) in enumerate(
            [(gq_buf, gq_hbm), (gk_buf, gk_hbm), (gv_buf, gv_hbm), (out_buf, out_hbm), (all_buf, gf_hbm)]
        )
    ]
    outs[0].start()
    back = jnp.where(
        lax.rem(lanes + sublanes + kernel_size // 2 + 1, kernel_size) == 0, 1.0, 0.0
    ).astype(f32)
    local_buf[...] = jnp.dot(local_buf[...], back, preferred_element_type=f32, precision=lax.Precision.HIGHEST)

    def owned(t):
        return pl.ds(pl.multiple_of(t * rows, rows), rows)

    def term_copy(t, slot):
        return remote(local_buf.at[owned(lax.rem(t, owners))], terms_buf.at[slot], term_send.at[t], term_recv.at[slot], tok=t)

    def sum_copy(t, owner):
        return remote(all_buf.at[owned(owner)], all_buf.at[owned(owner)], sum_send.at[t], sum_recv.at[owner], tok=t)

    def if_owner(t, action):
        if owners == n_tok:
            action()
        else:
            pl.when(t < owners)(action)

    for t in other_toks:
        if_owner(t, lambda t=t: term_copy(t, tok).start())

    def project(block, start, depth):
        deep = pl.ds(pl.multiple_of(block * width + start, depth), depth)
        return dot(gather[block, :, pl.ds(pl.multiple_of(start, depth), depth)], w_buf[deep, :])

    for h in range(pieces):
        own_copy(h, sibling).wait_recv()
    both = pl.ds(pl.multiple_of(chip * 2 * width, 2 * width), 2 * width)
    total[...] = dot(jnp.concatenate([gather[chip * 2], gather[chip * 2 + 1]], axis=1), w_buf[both, :])

    def sum_terms():
        for t in other_toks:
            term_copy(t, t).wait_recv()
        terms_buf[tok] = local_buf[owned(tok), :]
        all_buf[owned(tok), :] = jnp.sum(terms_buf[...], axis=0) * scale
        for t in other_toks:
            sum_copy(t, tok).start()

    if_owner(tok, sum_terms)

    @pl.when(jnp.logical_not(has_next))
    def _():
        gcn_t[...] = jnp.zeros_like(gcn_t)

    @pl.loop(0, pieces)
    def _(h):
        @pl.when(has_next)
        def _():
            gc_copy(h).wait_recv()

        keep = as_mask(lanes <= sublanes)
        for i in range(tiles):
            at = tile_of(h, i)
            grad_kv = conv_tile(frev_buf[groups_of(h, i), :], gc_t[at, :], gcn_t[at, :], keep, group_size).T
            gk_buf[:, at] = (grad_kv * v_ref[:, at].astype(f32)).astype(bf16)
            gv_buf[:, at] = (grad_kv * k_ref[:, at].astype(f32)).astype(bf16)

    outs[1].start()
    outs[2].start()

    def arrived(i):
        p, h = step_of(i)
        peer_copy(p, h, p * 2 + core, p).wait_recv()
        fwd_copy(p, h, p * 2 + core).start()

    def near_half(i):
        p, h = step_of(i)
        return project(p * 2 + core, h * piece, piece)

    def far_half(i):
        p, h = step_of(i)
        fwd_copy(p, h, p * 2 + 1 - core).wait_recv()
        return project(p * 2 + 1 - core, h * piece, piece)

    arrived(0)
    total[...] = total[...] + near_half(0)

    def add_step(j):
        arrived(j + 1)
        total[...] = total[...] + (far_half(j) + near_half(j + 1))

    each(steps - 1, add_step)
    out_buf[...] = (total[...] + far_half(steps - 1)).astype(bf16)
    outs[3].start()
    for t in other_toks:
        if_owner(t, lambda t=t: sum_copy(t, t).wait_recv())
    outs[4].start()

    for h in range(pieces):
        pl.when(has_next)(lambda h=h: kv_copy(h).wait_send())
        pl.when(has_previous)(lambda h=h: gc_copy(h).wait_send())
        sib_copy(chip, h).wait_send()
        own_copy(h, me).wait_send()

    @pl.loop(0, steps)
    def _(i):
        p, h = step_of(i)
        sib_copy(p, h).wait_send()
        pre_copy(p, chip, h).wait_send()
        peer_copy(p, h, me, chip).wait_send()
        fwd_copy(p, h, p * 2 + core).wait_send()

    for t in other_toks:
        if_owner(t, lambda t=t: term_copy(t, tok).wait_send())

    def sums_sent():
        for t in other_toks:
            sum_copy(t, tok).wait_send()

    if_owner(tok, sums_sent)
    for copy in outs:
        copy.wait()


def hand_on(*refs):
    count = (len(refs) - 2) // 3
    source, target, held = refs[:count], refs[count : 2 * count], refs[2 * count : 3 * count]
    in_sem, out_sem = refs[3 * count :]
    loads = [pltpu.make_async_copy(source[i], held[i], in_sem.at[i]) for i in range(count)]
    stores = [pltpu.make_async_copy(held[i], target[i], out_sem.at[i]) for i in range(count)]
    for copy in loads:
        copy.start()
    for load, store in zip(loads, stores):
        load.wait()
        store.start()
    for copy in stores:
        copy.wait()


def local(queries, key_branch, value_branch, filters, out_weight, cotangent):
    length, width = queries.shape
    groups, kernel_size = filters.shape
    n_tok, n_wid = lax.axis_size("tok"), lax.axis_size("wid")
    chips = n_wid // 2
    group_size = width // groups
    tile = min(128, width // 2)
    piece = max(tile, width // 4)
    pieces = width // piece
    owners = min(n_tok, groups // 8)
    wide = jax.ShapeDtypeStruct((length, width), bf16)
    results = [wide] * 4 + [jax.ShapeDtypeStruct(filters.shape, f32)]
    dma = pltpu.SemaphoreType.DMA
    hbm = pl.BlockSpec(memory_space=pl.ANY)
    flat, turned = pltpu.VMEM((length, width), bf16), pltpu.VMEM((width, length), bf16)
    turned_f32 = pltpu.VMEM((width, length), f32)
    by_chip = pltpu.VMEM((chips, width, length), bf16)
    taps = pltpu.VMEM(filters.shape, f32)
    scale = 1.0 / math.sqrt(length * n_tok * group_size)
    outs = pl.pallas_call(
        functools.partial(kernel, (n_tok, n_wid, tile, piece, owners), scale),
        in_specs=[hbm] * 6,
        out_specs=[hbm] * 5,
        out_shape=results,
        scratch_shapes=[
            flat, flat, flat, taps, flat,
            pltpu.VMEM(out_weight.shape, bf16),
            turned, turned, turned, turned, turned_f32, turned_f32,
            by_chip, by_chip, by_chip, by_chip,
            pltpu.VMEM((n_wid, length, width), bf16),
            pltpu.VMEM((length, width), f32),
            turned, turned,
            flat, flat, flat, flat,
            taps, taps,
            pltpu.VMEM((n_tok, groups // owners, kernel_size), f32),
            taps,
            dma((5,)), dma((5,)), dma((n_wid * pieces,)),
            dma((pieces,)), dma((pieces,)),
            dma((chips * pieces,)), dma((chips * pieces,)), dma((chips * pieces,)), dma((chips * pieces,)),
            dma((pieces,)), dma((pieces,)),
            dma((chips * pieces,)), dma((chips * pieces,)), dma((chips * pieces,)), dma((chips * pieces,)),
            dma((pieces,)), dma((pieces,)),
            dma((n_tok,)), dma((n_tok,)), dma((n_tok,)), dma((n_tok,)),
        ],
        compiler_params=pltpu.CompilerParams(
            collective_id=0, has_side_effects=True, vmem_limit_bytes=60 * 2**20
        ),
        cost_estimate=pl.CostEstimate(
            flops=4 * length * width * width * n_wid, bytes_accessed=2 * width * width * n_wid, transcendentals=0
        ),
    )(queries, key_branch, value_branch, filters, out_weight, cotangent)
    return pl.pallas_call(
        hand_on, in_specs=[hbm] * 5, out_specs=[hbm] * 5, out_shape=results, scratch_shapes=[flat] * 4 + [taps, dma((5,)), dma((5,))]
    )(*outs)


def solution(mesh):
    return jax.shard_map(
        local,
        mesh=mesh,
        in_specs=(
            P("tok", "wid"),
            P("tok", "wid"),
            P("tok", "wid"),
            P("wid", None),
            P(None, "wid"),
            P("tok", "wid"),
        ),
        out_specs=(
            P("tok", "wid"),
            P("tok", "wid"),
            P("tok", "wid"),
            P("tok", "wid"),
            P("wid", None),
        ),
        check_vma=False,
    )
```

```python
import functools
import math

import jax
import jax.numpy as jnp
from jax import lax
from jax.experimental import pallas as pl
from jax.experimental.pallas import tpu as pltpu
from jax.sharding import PartitionSpec as P

bf16, f32 = jnp.bfloat16, jnp.float32


def iota(shape, dim):
    return lax.broadcasted_iota(jnp.int32, shape, dim)


def as_mask(condition):
    return jnp.where(condition, 1.0, 0.0).astype(bf16)


def dot(a, b):
    return jnp.dot(a, b, preferred_element_type=f32)


def fanned(rows):
    return pltpu.roll(rows, 0, 1, stride=1, stride_axis=0)


def conv_tile(filters, own, other, keep, group_size):
    groups, kernel = filters.shape
    data = jnp.concatenate([own, other], axis=1)
    parts = []
    for g in range(groups):
        ring = fanned(jnp.broadcast_to(filters[g : g + 1], (kernel, kernel))).astype(bf16)
        kept = ring * keep
        taps = jnp.concatenate([kept, ring - kept], axis=0)
        parts.append(dot(data[g * group_size : (g + 1) * group_size], taps))
    return jnp.concatenate(parts, axis=0)


def filter_tile(before, own, turned, groups, group_size):
    tile, kernel = own.shape
    half = kernel // 2
    window = jnp.concatenate([before, own], axis=1)
    later = jnp.concatenate([window[:, half:], window[:, :half]], axis=1)
    data = jnp.concatenate([window, later], axis=0)
    turned = jnp.concatenate([turned[:half], turned[half:]], axis=1)
    owner = lax.rem(iota((half, 2 * tile), 1), tile) // group_size
    parts = dot(jnp.concatenate([turned * as_mask(owner == g) for g in range(groups)], axis=0), data)
    now = iota((half, kernel), 0) + iota((half, kernel), 1) <= half - 1
    rows = []
    for g in range(groups):
        part = parts[g * half : (g + 1) * half]
        square = jnp.where(now, part[:, kernel:], part[:, :kernel])
        rows.append(jnp.sum(fanned(square), axis=0, keepdims=True))
    return jnp.concatenate(rows, axis=0)


def each(count, body):
    if count <= 4:
        for i in range(count):
            body(i)
    else:
        pl.loop(0, count)(body)


def when(condition, action):
    if isinstance(condition, bool):
        if condition:
            action()
    else:
        pl.when(condition)(action)


def kernel(
    sizes, scale,
    q_hbm, k_hbm, v_hbm, f_hbm, w_hbm, cot_hbm,
    out_hbm, gq_hbm, gk_hbm, gv_hbm, gf_hbm,
    q_ref, k_ref, v_ref, f_ref, cot_ref, w_buf, cot_t, q_t, kv_t, rim_t, conv_t, part_t,
    sib_out, sib_in, pre_out, pre_in, gather, total, gc_t, gcn_t,
    out_buf, gq_buf, gk_buf, gv_buf, frev_buf, local_buf, terms_buf, all_buf,
    in_sem, out_sem, w_sem, kv_send, kv_recv, sib_send, sib_recv, pre_send, pre_recv,
    own_send, own_recv, peer_send, peer_recv, fwd_send, fwd_recv, gc_send, gc_recv,
    term_send, term_recv, sum_send, sum_recv,
):
    n_tok, n_wid, tile, piece, owners = sizes
    length, width = q_ref.shape
    groups, kernel_size = f_ref.shape
    group_size = width // groups
    tile_groups = tile // group_size
    pieces = width // piece
    tiles = piece // tile
    chips = n_wid // 2
    steps = (chips - 1) * pieces
    rows = groups // owners
    tok, me = lax.axis_index("tok"), lax.axis_index("wid")
    chip, core = me // 2, lax.rem(me, 2)
    sibling = chip * 2 + 1 - core
    other_chips = [lax.rem(chip + off, chips) for off in range(1, chips)]
    other_toks = [lax.rem(tok + off, n_tok) for off in range(1, n_tok)]
    has_next, has_previous = tok < n_tok - 1, tok > 0

    def step_of(i):
        return lax.rem(chip + 1 + i // pieces, chips), lax.rem(i, pieces)

    def span(h):
        return pl.ds(pl.multiple_of(h * piece, piece), piece)

    def tile_of(h, i):
        return pl.ds(pl.multiple_of(h * piece + i * tile, tile), tile)

    def groups_of(h, i):
        return pl.ds(pl.multiple_of((h * tiles + i) * tile_groups, tile_groups), tile_groups)

    ins = [
        pltpu.make_async_copy(src, dst, in_sem.at[i])
        for i, (src, dst) in enumerate(
            [(k_hbm, k_ref), (v_hbm, v_ref), (cot_hbm, cot_ref), (q_hbm, q_ref), (f_hbm, f_ref)]
        )
    ]
    for copy in ins[:3]:
        copy.start()

    def w_rows(block, h):
        return pl.ds(pl.multiple_of(block * width + h * piece, piece), piece)

    def w_copy(block, h):
        at = w_rows(block, h)
        return pltpu.make_async_copy(w_hbm.at[at], w_buf.at[at], w_sem.at[block * pieces + h])

    @pl.loop(0, steps)
    def _(i):
        p, h = step_of(i)
        w_copy(p * 2 + 1 - core, h).start()
        w_copy(p * 2 + core, h).start()

    for copy in ins[3:]:
        copy.start()
    for block in (sibling, me):

        @pl.loop(0, pieces)
        def _(h):
            w_copy(block, h).start()

    def remote(src, dst, send, recv, **where):
        return pltpu.make_async_remote_copy(
            src_ref=src, dst_ref=dst, send_sem=send, recv_sem=recv,
            device_id=where, device_id_type=pl.DeviceIdType.MESH,
        )

    barrier = pltpu.get_barrier_semaphore()
    for where in (
        [{"wid": sibling}] + [{"wid": p * 2 + core} for p in other_chips] + [{"tok": t} for t in other_toks]
    ):
        pl.semaphore_signal(barrier, inc=1, device_id=where, device_id_type=pl.DeviceIdType.MESH)

    ins[0].wait()
    ins[1].wait()

    @pl.loop(0, pieces)
    def _(h):
        for i in range(tiles):
            at = tile_of(h, i)
            kv_t[at, :] = (k_ref[:, at].astype(f32) * v_ref[:, at].astype(f32)).astype(bf16).T

    ins[2].wait()

    @pl.loop(0, pieces)
    def _(h):
        for i in range(tiles):
            at = tile_of(h, i)
            cot_t[at, :] = cot_ref[:, at].T

    def turn_queries():
        for i in range(width // tile):
            at = pl.ds(i * tile, tile)
            q_t[at, :] = q_ref[:, at].T

    def kv_copy(h):
        return remote(
            kv_t.at[span(h)], rim_t.at[span(h)], kv_send.at[h], kv_recv.at[h], tok=lax.rem(tok + 1, n_tok)
        )

    def gc_copy(h):
        return remote(
            gc_t.at[span(h)], gcn_t.at[span(h)], gc_send.at[h], gc_recv.at[h], tok=lax.rem(tok + n_tok - 1, n_tok)
        )

    def sib_copy(p, h):
        sem = p * pieces + h
        return remote(
            sib_out.at[p, span(h)], sib_in.at[p, span(h)], sib_send.at[sem], sib_recv.at[sem], wid=sibling
        )

    def pre_copy(p, slot, h):
        return remote(
            pre_out.at[p, span(h)], pre_in.at[slot, span(h)],
            pre_send.at[p * pieces + h], pre_recv.at[slot * pieces + h], wid=p * 2 + core,
        )

    def send_sum(i):
        p, h = step_of(i)
        sib_copy(p, h).wait_recv()
        pre_out[p, span(h), :] = (part_t[span(h), :] + sib_in[p, span(h), :].astype(f32)).astype(bf16)
        pre_copy(p, chip, h).start()

    def two_parts(i):
        p, h = step_of(i)
        w_copy(p * 2 + 1 - core, h).wait()
        w_copy(p * 2 + core, h).wait()
        sib_out[p, span(h), :] = dot(w_buf[w_rows(p * 2 + 1 - core, h), :], cot_t[...]).astype(bf16)
        part_t[span(h), :] = dot(w_buf[w_rows(p * 2 + core, h), :], cot_t[...])

    def own_parts(block, store):
        for h in range(pieces):
            w_copy(block, h).wait()
        size = 2 * piece if pieces % 2 == 0 else piece
        for start in range(0, width, size):
            rows_at = pl.ds(pl.multiple_of(block * width + start, size), size)
            store(pl.ds(start, size), dot(w_buf[rows_at, :], cot_t[...]))

    pl.semaphore_wait(barrier, 1 + len(other_chips) + len(other_toks))

    @pl.when(has_next)
    def _():
        for h in range(pieces):
            kv_copy(h).start()

    two_parts(0)
    sib_copy(*step_of(0)).start()

    def sum_step(j):
        i = j + 1
        if pieces > 1:
            two_parts(i)
            sib_copy(*step_of(i)).start()
            send_sum(i - 1)
        else:
            send_sum(i - 1)
            two_parts(i)
            sib_copy(*step_of(i)).start()

    each(steps - 1, sum_step)

    def store_sibling(at, product):
        sib_out[chip, at, :] = product.astype(bf16)

    own_parts(sibling, store_sibling)
    for h in range(pieces):
        sib_copy(chip, h).start()
    send_sum(steps - 1)

    ins[3].wait()
    ins[4].wait()
    lanes, sublanes = iota((kernel_size, kernel_size), 1), iota((kernel_size, kernel_size), 0)
    flip = as_mask(lax.rem(lanes + sublanes, kernel_size) == 0)
    frev_buf[...] = dot(f_ref[...].astype(bf16), flip)

    def own_copy(h, slot):
        return remote(
            gather.at[me, :, span(h)], gather.at[slot, :, span(h)], own_send.at[h], own_recv.at[h], wid=sibling
        )

    def peer_copy(p, h, slot, slot_chip):
        return remote(
            gather.at[me, :, span(h)], gather.at[slot, :, span(h)],
            peer_send.at[p * pieces + h], peer_recv.at[slot_chip * pieces + h], wid=p * 2 + core,
        )

    def fwd_copy(p, h, slot):
        return remote(
            gather.at[p * 2 + core, :, span(h)], gather.at[slot, :, span(h)],
            fwd_send.at[p * pieces + h], fwd_recv.at[p * pieces + h], wid=sibling,
        )

    @pl.when(jnp.logical_not(has_previous))
    def _():
        rim_t[...] = jnp.zeros_like(rim_t)

    def forward_piece(h):
        @pl.when(has_previous)
        def _():
            kv_copy(h).wait_recv()

        keep = as_mask(sublanes <= lanes)
        for i in range(tiles):
            at = tile_of(h, i)
            conv = conv_tile(f_ref[groups_of(h, i), :], kv_t[at, :], rim_t[at, :], keep, group_size)
            conv_t[at, :] = conv
            gather[me, :, at] = (q_t[at, :].astype(f32) * conv).astype(bf16).T
        for p in other_chips:
            peer_copy(p, h, me, chip).start()
        own_copy(h, me).start()

    def store_own(at, product):
        part_t[at, :] = product

    turn_queries()
    own_parts(me, store_own)

    mirror = as_mask(
        jnp.logical_and(
            lanes // (kernel_size // 2) == sublanes // (kernel_size // 2),
            lax.rem(lanes, kernel_size // 2) + lax.rem(sublanes, kernel_size // 2) == kernel_size // 2 - 1,
        )
    )

    def grad_piece(h):
        sib_copy(chip, h).wait_recv()
        for p in other_chips:
            pre_copy(p, p, h).wait_recv()
        at = span(h)
        grad_gated = part_t[at, :] + sib_in[chip, at, :].astype(f32)
        for p in other_chips:
            grad_gated = grad_gated + pre_in[p, at, :].astype(f32)
        gc_t[at, :] = (grad_gated * q_t[at, :].astype(f32)).astype(bf16)
        part_t[at, :] = grad_gated

    def send_grads(which):
        @pl.when(has_previous)
        def _():
            for h in which:
                gc_copy(h).start()

    def filter_piece(h):
        turned = []
        for i in range(tiles):
            at = tile_of(h, i)
            gq_buf[:, at] = (part_t[at, :] * conv_t[at, :]).astype(bf16).T
            turned.append(gc_t[at, :].T)
        turned = dot(mirror, jnp.concatenate(turned, axis=1)).astype(bf16)
        for i in range(tiles):
            at = tile_of(h, i)
            local_buf[groups_of(h, i), :] = filter_tile(
                rim_t[at, :], kv_t[at, :], turned[:, i * tile : (i + 1) * tile], tile_groups, group_size
            )

    for h in range(pieces):
        forward_piece(h)
    first = max(pieces - 2, 0)
    for h in range(pieces):
        grad_piece(h)
        if h < first:
            send_grads([h])
    for h in range(pieces):
        filter_piece(h)

    outs = [
        pltpu.make_async_copy(src, dst, out_sem.at[i])
        for i, (src, dst) in enumerate(
            [(gq_buf, gq_hbm), (gk_buf, gk_hbm), (gv_buf, gv_hbm), (out_buf, out_hbm), (all_buf, gf_hbm)]
        )
    ]
    outs[0].start()
    back = jnp.where(
        lax.rem(lanes + sublanes + kernel_size // 2 + 1, kernel_size) == 0, 1.0, 0.0
    ).astype(f32)
    local_buf[...] = jnp.dot(local_buf[...], back, preferred_element_type=f32, precision=lax.Precision.HIGHEST)

    def owned(t):
        return pl.ds(pl.multiple_of(t * rows, rows), rows)

    def term_copy(t, slot):
        return remote(local_buf.at[owned(lax.rem(t, owners))], terms_buf.at[slot], term_send.at[t], term_recv.at[slot], tok=t)

    def sum_copy(t, owner):
        return remote(all_buf.at[owned(owner)], all_buf.at[owned(owner)], sum_send.at[t], sum_recv.at[owner], tok=t)

    def if_owner(t, action):
        if owners == n_tok:
            action()
        else:
            pl.when(t < owners)(action)

    for t in other_toks:
        if_owner(t, lambda t=t: term_copy(t, tok).start())
    send_grads(range(first, pieces))

    def project(block, start, depth):
        deep = pl.ds(pl.multiple_of(block * width + start, depth), depth)
        return dot(gather[block, :, pl.ds(pl.multiple_of(start, depth), depth)], w_buf[deep, :])

    for h in range(pieces):
        own_copy(h, sibling).wait_recv()
    both = pl.ds(pl.multiple_of(chip * 2 * width, 2 * width), 2 * width)
    total[...] = dot(jnp.concatenate([gather[chip * 2], gather[chip * 2 + 1]], axis=1), w_buf[both, :])

    def sum_terms():
        for t in other_toks:
            term_copy(t, t).wait_recv()
        terms_buf[tok] = local_buf[owned(tok), :]
        all_buf[owned(tok), :] = jnp.sum(terms_buf[...], axis=0) * scale
        for t in other_toks:
            sum_copy(t, tok).start()


    @pl.when(jnp.logical_not(has_next))
    def _():
        gcn_t[...] = jnp.zeros_like(gcn_t)

    def back_piece(h):
        @pl.when(has_next)
        def _():
            gc_copy(h).wait_recv()

        keep = as_mask(lanes <= sublanes)
        for i in range(tiles):
            at = tile_of(h, i)
            grad_kv = conv_tile(frev_buf[groups_of(h, i), :], gc_t[at, :], gcn_t[at, :], keep, group_size).T
            gk_buf[:, at] = (grad_kv * v_ref[:, at].astype(f32)).astype(bf16)
            gv_buf[:, at] = (grad_kv * k_ref[:, at].astype(f32)).astype(bf16)

    def arrived(i):
        p, h = step_of(i)
        peer_copy(p, h, p * 2 + core, p).wait_recv()
        fwd_copy(p, h, p * 2 + core).start()

    def near_half(i):
        p, h = step_of(i)
        return project(p * 2 + core, h * piece, piece)

    def far_half(i):
        p, h = step_of(i)
        fwd_copy(p, h, p * 2 + 1 - core).wait_recv()
        return project(p * 2 + 1 - core, h * piece, piece)

    mixed = steps == pieces
    back_piece(0)
    arrived(0)
    total[...] = total[...] + near_half(0)

    def add_step(j):
        if mixed:
            back_piece(j + 1)
        arrived(j + 1)
        total[...] = total[...] + (far_half(j) + near_half(j + 1))

    if not mixed:
        for h in range(1, pieces):
            back_piece(h)
    early = max(steps - 3, 0) if mixed else 0
    each(early, add_step)
    if_owner(tok, sum_terms)
    if mixed:
        for j in range(early, steps - 1):
            add_step(j)
    else:
        each(steps - 1, add_step)
    outs[1].start()
    outs[2].start()
    out_buf[...] = (total[...] + far_half(steps - 1)).astype(bf16)
    outs[3].start()
    for t in other_toks:
        if_owner(t, lambda t=t: sum_copy(t, t).wait_recv())
    outs[4].start()

    for h in range(pieces):
        pl.when(has_next)(lambda h=h: kv_copy(h).wait_send())
        pl.when(has_previous)(lambda h=h: gc_copy(h).wait_send())
        sib_copy(chip, h).wait_send()
        own_copy(h, me).wait_send()

    @pl.loop(0, steps)
    def _(i):
        p, h = step_of(i)
        sib_copy(p, h).wait_send()
        pre_copy(p, chip, h).wait_send()
        peer_copy(p, h, me, chip).wait_send()
        fwd_copy(p, h, p * 2 + core).wait_send()

    for t in other_toks:
        if_owner(t, lambda t=t: term_copy(t, tok).wait_send())

    def sums_sent():
        for t in other_toks:
            sum_copy(t, tok).wait_send()

    if_owner(tok, sums_sent)
    for copy in outs:
        copy.wait()


def hand_on(*refs):
    count = (len(refs) - 2) // 3
    source, target, held = refs[:count], refs[count : 2 * count], refs[2 * count : 3 * count]
    in_sem, out_sem = refs[3 * count :]
    loads = [pltpu.make_async_copy(source[i], held[i], in_sem.at[i]) for i in range(count)]
    stores = [pltpu.make_async_copy(held[i], target[i], out_sem.at[i]) for i in range(count)]
    for copy in loads:
        copy.start()
    for load, store in zip(loads, stores):
        load.wait()
        store.start()
    for copy in stores:
        copy.wait()


def local(queries, key_branch, value_branch, filters, out_weight, cotangent):
    length, width = queries.shape
    groups, kernel_size = filters.shape
    n_tok, n_wid = lax.axis_size("tok"), lax.axis_size("wid")
    chips = n_wid // 2
    group_size = width // groups
    tile = min(128, width // 2)
    piece = max(tile, width // 4)
    pieces = width // piece
    owners = min(n_tok, groups // 8)
    wide = jax.ShapeDtypeStruct((length, width), bf16)
    results = [wide] * 4 + [jax.ShapeDtypeStruct(filters.shape, f32)]
    dma = pltpu.SemaphoreType.DMA
    hbm = pl.BlockSpec(memory_space=pl.ANY)
    flat, turned = pltpu.VMEM((length, width), bf16), pltpu.VMEM((width, length), bf16)
    turned_f32 = pltpu.VMEM((width, length), f32)
    by_chip = pltpu.VMEM((chips, width, length), bf16)
    taps = pltpu.VMEM(filters.shape, f32)
    scale = 1.0 / math.sqrt(length * n_tok * group_size)
    outs = pl.pallas_call(
        functools.partial(kernel, (n_tok, n_wid, tile, piece, owners), scale),
        in_specs=[hbm] * 6,
        out_specs=[hbm] * 5,
        out_shape=results,
        scratch_shapes=[
            flat, flat, flat, taps, flat,
            pltpu.VMEM(out_weight.shape, bf16),
            turned, turned, turned, turned, turned_f32, turned_f32,
            by_chip, by_chip, by_chip, by_chip,
            pltpu.VMEM((n_wid, length, width), bf16),
            pltpu.VMEM((length, width), f32),
            turned, turned,
            flat, flat, flat, flat,
            taps, taps,
            pltpu.VMEM((n_tok, groups // owners, kernel_size), f32),
            taps,
            dma((5,)), dma((5,)), dma((n_wid * pieces,)),
            dma((pieces,)), dma((pieces,)),
            dma((chips * pieces,)), dma((chips * pieces,)), dma((chips * pieces,)), dma((chips * pieces,)),
            dma((pieces,)), dma((pieces,)),
            dma((chips * pieces,)), dma((chips * pieces,)), dma((chips * pieces,)), dma((chips * pieces,)),
            dma((pieces,)), dma((pieces,)),
            dma((n_tok,)), dma((n_tok,)), dma((n_tok,)), dma((n_tok,)),
        ],
        compiler_params=pltpu.CompilerParams(
            collective_id=0, has_side_effects=True, vmem_limit_bytes=60 * 2**20
        ),
        cost_estimate=pl.CostEstimate(
            flops=4 * length * width * width * n_wid, bytes_accessed=2 * width * width * n_wid, transcendentals=0
        ),
    )(queries, key_branch, value_branch, filters, out_weight, cotangent)
    return pl.pallas_call(
        hand_on, in_specs=[hbm] * 5, out_specs=[hbm] * 5, out_shape=results, scratch_shapes=[flat] * 4 + [taps, dma((5,)), dma((5,))]
    )(*outs)


def solution(mesh):
    return jax.shard_map(
        local,
        mesh=mesh,
        in_specs=(
            P("tok", "wid"),
            P("tok", "wid"),
            P("tok", "wid"),
            P("wid", None),
            P(None, "wid"),
            P("tok", "wid"),
        ),
        out_specs=(
            P("tok", "wid"),
            P("tok", "wid"),
            P("tok", "wid"),
            P("tok", "wid"),
            P("wid", None),
        ),
        check_vma=False,
    )
```

```python
import functools
import math

import jax
import jax.numpy as jnp
from jax import lax
from jax.experimental import pallas as pl
from jax.experimental.pallas import tpu as pltpu
from jax.sharding import PartitionSpec as P

bf16, f32 = jnp.bfloat16, jnp.float32


def iota(shape, dim):
    return lax.broadcasted_iota(jnp.int32, shape, dim)


def as_mask(condition):
    return jnp.where(condition, 1.0, 0.0).astype(bf16)


def dot(a, b):
    return jnp.dot(a, b, preferred_element_type=f32)


def fanned(rows):
    return pltpu.roll(rows, 0, 1, stride=1, stride_axis=0)


def conv_tile(filters, own, other, keep, group_size):
    groups, kernel = filters.shape
    data = jnp.concatenate([own, other], axis=1)
    parts = []
    for g in range(groups):
        ring = fanned(jnp.broadcast_to(filters[g : g + 1], (kernel, kernel))).astype(bf16)
        kept = ring * keep
        taps = jnp.concatenate([kept, ring - kept], axis=0)
        parts.append(dot(data[g * group_size : (g + 1) * group_size], taps))
    return jnp.concatenate(parts, axis=0)


def filter_tile(before, own, turned, groups, group_size):
    tile, kernel = own.shape
    half = kernel // 2
    window = jnp.concatenate([before, own], axis=1)
    later = jnp.concatenate([window[:, half:], window[:, :half]], axis=1)
    data = jnp.concatenate([window, later], axis=0)
    turned = jnp.concatenate([turned[:half], turned[half:]], axis=1)
    owner = lax.rem(iota((half, 2 * tile), 1), tile) // group_size
    parts = dot(jnp.concatenate([turned * as_mask(owner == g) for g in range(groups)], axis=0), data)
    now = iota((half, kernel), 0) + iota((half, kernel), 1) <= half - 1
    rows = []
    for g in range(groups):
        part = parts[g * half : (g + 1) * half]
        square = jnp.where(now, part[:, kernel:], part[:, :kernel])
        rows.append(jnp.sum(fanned(square), axis=0, keepdims=True))
    return jnp.concatenate(rows, axis=0)


def each(count, body):
    if count <= 4:
        for i in range(count):
            body(i)
    else:
        pl.loop(0, count)(body)


def when(condition, action):
    if isinstance(condition, bool):
        if condition:
            action()
    else:
        pl.when(condition)(action)


def kernel(
    sizes, scale,
    q_hbm, k_hbm, v_hbm, f_hbm, w_hbm, cot_hbm,
    out_hbm, gq_hbm, gk_hbm, gv_hbm, gf_hbm,
    q_ref, k_ref, v_ref, f_ref, cot_ref, w_buf, cot_t, q_t, kv_t, rim_t, conv_t, part_t,
    sib_out, sib_in, pre_out, pre_in, gather, total, gc_t, gcn_t,
    out_buf, gq_buf, gk_buf, gv_buf, frev_buf, local_buf, terms_buf, all_buf,
    in_sem, out_sem, w_sem, kv_send, kv_recv, sib_send, sib_recv, pre_send, pre_recv,
    own_send, own_recv, peer_send, peer_recv, fwd_send, fwd_recv, gc_send, gc_recv,
    term_send, term_recv, sum_send, sum_recv,
):
    n_tok, n_wid, tile, piece, owners = sizes
    length, width = q_ref.shape
    groups, kernel_size = f_ref.shape
    group_size = width // groups
    tile_groups = tile // group_size
    pieces = width // piece
    tiles = piece // tile
    chips = n_wid // 2
    steps = (chips - 1) * pieces
    rows = groups // owners
    tok, me = lax.axis_index("tok"), lax.axis_index("wid")
    chip, core = me // 2, lax.rem(me, 2)
    sibling = chip * 2 + 1 - core
    other_chips = [lax.rem(chip + off, chips) for off in range(1, chips)]
    other_toks = [lax.rem(tok + off, n_tok) for off in range(1, n_tok)]
    has_next, has_previous = tok < n_tok - 1, tok > 0

    def step_of(i):
        return lax.rem(chip + 1 + i // pieces, chips), lax.rem(i, pieces)

    def span(h):
        return pl.ds(pl.multiple_of(h * piece, piece), piece)

    def tile_of(h, i):
        return pl.ds(pl.multiple_of(h * piece + i * tile, tile), tile)

    def groups_of(h, i):
        return pl.ds(pl.multiple_of((h * tiles + i) * tile_groups, tile_groups), tile_groups)

    ins = [
        pltpu.make_async_copy(src, dst, in_sem.at[i])
        for i, (src, dst) in enumerate(
            [(k_hbm, k_ref), (v_hbm, v_ref), (cot_hbm, cot_ref), (q_hbm, q_ref), (f_hbm, f_ref)]
        )
    ]
    for copy in ins[:3]:
        copy.start()

    def w_rows(block, h):
        return pl.ds(pl.multiple_of(block * width + h * piece, piece), piece)

    def w_copy(block, h):
        at = w_rows(block, h)
        return pltpu.make_async_copy(w_hbm.at[at], w_buf.at[at], w_sem.at[block * pieces + h])

    @pl.loop(0, steps)
    def _(i):
        p, h = step_of(i)
        w_copy(p * 2 + 1 - core, h).start()
        w_copy(p * 2 + core, h).start()

    for copy in ins[3:]:
        copy.start()
    for block in (sibling, me):

        @pl.loop(0, pieces)
        def _(h):
            w_copy(block, h).start()

    def remote(src, dst, send, recv, **where):
        return pltpu.make_async_remote_copy(
            src_ref=src, dst_ref=dst, send_sem=send, recv_sem=recv,
            device_id=where, device_id_type=pl.DeviceIdType.MESH,
        )

    barrier = pltpu.get_barrier_semaphore()
    for where in (
        [{"wid": sibling}] + [{"wid": p * 2 + core} for p in other_chips] + [{"tok": t} for t in other_toks]
    ):
        pl.semaphore_signal(barrier, inc=1, device_id=where, device_id_type=pl.DeviceIdType.MESH)

    ins[0].wait()
    ins[1].wait()

    @pl.loop(0, pieces)
    def _(h):
        for i in range(tiles):
            at = tile_of(h, i)
            kv_t[at, :] = (k_ref[:, at].astype(f32) * v_ref[:, at].astype(f32)).astype(bf16).T

    ins[2].wait()

    @pl.loop(0, pieces)
    def _(h):
        for i in range(tiles):
            at = tile_of(h, i)
            cot_t[at, :] = cot_ref[:, at].T

    def turn_queries():
        for i in range(width // tile):
            at = pl.ds(i * tile, tile)
            q_t[at, :] = q_ref[:, at].T

    def kv_copy(h):
        return remote(
            kv_t.at[span(h)], rim_t.at[span(h)], kv_send.at[h], kv_recv.at[h], tok=lax.rem(tok + 1, n_tok)
        )

    def gc_copy(h):
        return remote(
            gc_t.at[span(h)], gcn_t.at[span(h)], gc_send.at[h], gc_recv.at[h], tok=lax.rem(tok + n_tok - 1, n_tok)
        )

    def sib_copy(p, h):
        sem = p * pieces + h
        return remote(
            sib_out.at[p, span(h)], sib_in.at[p, span(h)], sib_send.at[sem], sib_recv.at[sem], wid=sibling
        )

    def pre_copy(p, slot, h):
        return remote(
            pre_out.at[p, span(h)], pre_in.at[slot, span(h)],
            pre_send.at[p * pieces + h], pre_recv.at[slot * pieces + h], wid=p * 2 + core,
        )

    def send_sum(i):
        p, h = step_of(i)
        sib_copy(p, h).wait_recv()
        pre_out[p, span(h), :] = (part_t[span(h), :] + sib_in[p, span(h), :].astype(f32)).astype(bf16)
        pre_copy(p, chip, h).start()

    def two_parts(i):
        p, h = step_of(i)
        w_copy(p * 2 + 1 - core, h).wait()
        w_copy(p * 2 + core, h).wait()
        sib_out[p, span(h), :] = dot(w_buf[w_rows(p * 2 + 1 - core, h), :], cot_t[...]).astype(bf16)
        part_t[span(h), :] = dot(w_buf[w_rows(p * 2 + core, h), :], cot_t[...])

    def own_parts(block, store):
        for h in range(pieces):
            w_copy(block, h).wait()
        size = 2 * piece if pieces % 2 == 0 else piece
        for start in range(0, width, size):
            rows_at = pl.ds(pl.multiple_of(block * width + start, size), size)
            store(pl.ds(start, size), dot(w_buf[rows_at, :], cot_t[...]))

    pl.semaphore_wait(barrier, 1 + len(other_chips) + len(other_toks))

    @pl.when(has_next)
    def _():
        for h in range(pieces):
            kv_copy(h).start()

    two_parts(0)
    sib_copy(*step_of(0)).start()

    def sum_step(j):
        i = j + 1
        if pieces > 1:
            two_parts(i)
            sib_copy(*step_of(i)).start()
            send_sum(i - 1)
        else:
            send_sum(i - 1)
            two_parts(i)
            sib_copy(*step_of(i)).start()

    each(steps - 1, sum_step)

    def store_sibling(at, product):
        sib_out[chip, at, :] = product.astype(bf16)

    own_parts(sibling, store_sibling)
    for h in range(pieces):
        sib_copy(chip, h).start()
    send_sum(steps - 1)

    ins[3].wait()
    ins[4].wait()
    lanes, sublanes = iota((kernel_size, kernel_size), 1), iota((kernel_size, kernel_size), 0)
    flip = as_mask(lax.rem(lanes + sublanes, kernel_size) == 0)
    frev_buf[...] = dot(f_ref[...].astype(bf16), flip)

    def own_copy(h, slot):
        return remote(
            gather.at[me, :, span(h)], gather.at[slot, :, span(h)], own_send.at[h], own_recv.at[h], wid=sibling
        )

    def peer_copy(p, h, slot, slot_chip):
        return remote(
            gather.at[me, :, span(h)], gather.at[slot, :, span(h)],
            peer_send.at[p * pieces + h], peer_recv.at[slot_chip * pieces + h], wid=p * 2 + core,
        )

    def fwd_copy(p, h, slot):
        return remote(
            gather.at[p * 2 + core, :, span(h)], gather.at[slot, :, span(h)],
            fwd_send.at[p * pieces + h], fwd_recv.at[p * pieces + h], wid=sibling,
        )

    @pl.when(jnp.logical_not(has_previous))
    def _():
        rim_t[...] = jnp.zeros_like(rim_t)

    def forward_piece(h):
        @pl.when(has_previous)
        def _():
            kv_copy(h).wait_recv()

        keep = as_mask(sublanes <= lanes)
        for i in range(tiles):
            at = tile_of(h, i)
            conv = conv_tile(f_ref[groups_of(h, i), :], kv_t[at, :], rim_t[at, :], keep, group_size)
            conv_t[at, :] = conv
            gather[me, :, at] = (q_t[at, :].astype(f32) * conv).astype(bf16).T
        for p in other_chips:
            peer_copy(p, h, me, chip).start()
        own_copy(h, me).start()

    def store_own(at, product):
        part_t[at, :] = product

    turn_queries()
    own_parts(me, store_own)

    mirror = as_mask(
        jnp.logical_and(
            lanes // (kernel_size // 2) == sublanes // (kernel_size // 2),
            lax.rem(lanes, kernel_size // 2) + lax.rem(sublanes, kernel_size // 2) == kernel_size // 2 - 1,
        )
    )

    def grad_piece(h):
        sib_copy(chip, h).wait_recv()
        for p in other_chips:
            pre_copy(p, p, h).wait_recv()
        at = span(h)
        grad_gated = part_t[at, :] + sib_in[chip, at, :].astype(f32)
        for p in other_chips:
            grad_gated = grad_gated + pre_in[p, at, :].astype(f32)
        gc_t[at, :] = (grad_gated * q_t[at, :].astype(f32)).astype(bf16)
        part_t[at, :] = grad_gated

    def send_grads(which):
        @pl.when(has_previous)
        def _():
            for h in which:
                gc_copy(h).start()

    def filter_piece(h):
        turned = []
        for i in range(tiles):
            at = tile_of(h, i)
            gq_buf[:, at] = (part_t[at, :] * conv_t[at, :]).astype(bf16).T
            turned.append(gc_t[at, :].T)
        turned = dot(mirror, jnp.concatenate(turned, axis=1)).astype(bf16)
        for i in range(tiles):
            at = tile_of(h, i)
            local_buf[groups_of(h, i), :] = filter_tile(
                rim_t[at, :], kv_t[at, :], turned[:, i * tile : (i + 1) * tile], tile_groups, group_size
            )

    first = max(pieces - 2, 0)
    for h in range(pieces - 1):
        forward_piece(h)
    for h in range(pieces):
        grad_piece(h)
        if h == 0:
            forward_piece(pieces - 1)
        if h < first:
            send_grads([h])
    for h in range(pieces):
        filter_piece(h)

    outs = [
        pltpu.make_async_copy(src, dst, out_sem.at[i])
        for i, (src, dst) in enumerate(
            [(gq_buf, gq_hbm), (gk_buf, gk_hbm), (gv_buf, gv_hbm), (out_buf, out_hbm), (all_buf, gf_hbm)]
        )
    ]
    outs[0].start()
    back = jnp.where(
        lax.rem(lanes + sublanes + kernel_size // 2 + 1, kernel_size) == 0, 1.0, 0.0
    ).astype(f32)
    local_buf[...] = jnp.dot(local_buf[...], back, preferred_element_type=f32, precision=lax.Precision.HIGHEST)

    def owned(t):
        return pl.ds(pl.multiple_of(t * rows, rows), rows)

    def term_copy(t, slot):
        return remote(local_buf.at[owned(lax.rem(t, owners))], terms_buf.at[slot], term_send.at[t], term_recv.at[slot], tok=t)

    def sum_copy(t, owner):
        return remote(all_buf.at[owned(owner)], all_buf.at[owned(owner)], sum_send.at[t], sum_recv.at[owner], tok=t)

    def if_owner(t, action):
        if owners == n_tok:
            action()
        else:
            pl.when(t < owners)(action)

    for t in other_toks:
        if_owner(t, lambda t=t: term_copy(t, tok).start())
    send_grads(range(first, pieces))

    def project(block, start, depth):
        deep = pl.ds(pl.multiple_of(block * width + start, depth), depth)
        return dot(gather[block, :, pl.ds(pl.multiple_of(start, depth), depth)], w_buf[deep, :])

    for h in range(pieces):
        own_copy(h, sibling).wait_recv()
    both = pl.ds(pl.multiple_of(chip * 2 * width, 2 * width), 2 * width)
    total[...] = dot(jnp.concatenate([gather[chip * 2], gather[chip * 2 + 1]], axis=1), w_buf[both, :])

    def sum_terms():
        for t in other_toks:
            term_copy(t, t).wait_recv()
        terms_buf[tok] = local_buf[owned(tok), :]
        all_buf[owned(tok), :] = jnp.sum(terms_buf[...], axis=0) * scale
        for t in other_toks:
            sum_copy(t, tok).start()


    @pl.when(jnp.logical_not(has_next))
    def _():
        gcn_t[...] = jnp.zeros_like(gcn_t)

    def back_piece(h):
        @pl.when(has_next)
        def _():
            gc_copy(h).wait_recv()

        keep = as_mask(lanes <= sublanes)
        for i in range(tiles):
            at = tile_of(h, i)
            grad_kv = conv_tile(frev_buf[groups_of(h, i), :], gc_t[at, :], gcn_t[at, :], keep, group_size).T
            gk_buf[:, at] = (grad_kv * v_ref[:, at].astype(f32)).astype(bf16)
            gv_buf[:, at] = (grad_kv * k_ref[:, at].astype(f32)).astype(bf16)

    def arrived(i):
        p, h = step_of(i)
        peer_copy(p, h, p * 2 + core, p).wait_recv()
        fwd_copy(p, h, p * 2 + core).start()

    def near_half(i):
        p, h = step_of(i)
        return project(p * 2 + core, h * piece, piece)

    def far_half(i):
        p, h = step_of(i)
        fwd_copy(p, h, p * 2 + 1 - core).wait_recv()
        return project(p * 2 + 1 - core, h * piece, piece)

    mixed = steps == pieces
    back_piece(0)
    arrived(0)
    total[...] = total[...] + near_half(0)

    def add_step(j):
        if mixed:
            back_piece(j + 1)
        arrived(j + 1)
        total[...] = total[...] + (far_half(j) + near_half(j + 1))

    if not mixed:
        for h in range(1, pieces):
            back_piece(h)
    early = max(steps - 3, 0) if mixed else 0
    each(early, add_step)
    if_owner(tok, sum_terms)
    if mixed:
        for j in range(early, steps - 1):
            add_step(j)
    else:
        each(steps - 1, add_step)
    outs[1].start()
    outs[2].start()
    out_buf[...] = (total[...] + far_half(steps - 1)).astype(bf16)
    outs[3].start()
    for t in other_toks:
        if_owner(t, lambda t=t: sum_copy(t, t).wait_recv())
    outs[4].start()

    for h in range(pieces):
        pl.when(has_next)(lambda h=h: kv_copy(h).wait_send())
        pl.when(has_previous)(lambda h=h: gc_copy(h).wait_send())
        sib_copy(chip, h).wait_send()
        own_copy(h, me).wait_send()

    @pl.loop(0, steps)
    def _(i):
        p, h = step_of(i)
        sib_copy(p, h).wait_send()
        pre_copy(p, chip, h).wait_send()
        peer_copy(p, h, me, chip).wait_send()
        fwd_copy(p, h, p * 2 + core).wait_send()

    for t in other_toks:
        if_owner(t, lambda t=t: term_copy(t, tok).wait_send())

    def sums_sent():
        for t in other_toks:
            sum_copy(t, tok).wait_send()

    if_owner(tok, sums_sent)
    for copy in outs:
        copy.wait()


def hand_on(*refs):
    count = (len(refs) - 2) // 3
    source, target, held = refs[:count], refs[count : 2 * count], refs[2 * count : 3 * count]
    in_sem, out_sem = refs[3 * count :]
    loads = [pltpu.make_async_copy(source[i], held[i], in_sem.at[i]) for i in range(count)]
    stores = [pltpu.make_async_copy(held[i], target[i], out_sem.at[i]) for i in range(count)]
    for copy in loads:
        copy.start()
    for load, store in zip(loads, stores):
        load.wait()
        store.start()
    for copy in stores:
        copy.wait()


def local(queries, key_branch, value_branch, filters, out_weight, cotangent):
    length, width = queries.shape
    groups, kernel_size = filters.shape
    n_tok, n_wid = lax.axis_size("tok"), lax.axis_size("wid")
    chips = n_wid // 2
    group_size = width // groups
    tile = min(128, width // 2)
    piece = max(tile, width // 4)
    pieces = width // piece
    owners = min(n_tok, groups // 8)
    wide = jax.ShapeDtypeStruct((length, width), bf16)
    results = [wide] * 4 + [jax.ShapeDtypeStruct(filters.shape, f32)]
    dma = pltpu.SemaphoreType.DMA
    hbm = pl.BlockSpec(memory_space=pl.ANY)
    flat, turned = pltpu.VMEM((length, width), bf16), pltpu.VMEM((width, length), bf16)
    turned_f32 = pltpu.VMEM((width, length), f32)
    by_chip = pltpu.VMEM((chips, width, length), bf16)
    taps = pltpu.VMEM(filters.shape, f32)
    scale = 1.0 / math.sqrt(length * n_tok * group_size)
    outs = pl.pallas_call(
        functools.partial(kernel, (n_tok, n_wid, tile, piece, owners), scale),
        in_specs=[hbm] * 6,
        out_specs=[hbm] * 5,
        out_shape=results,
        scratch_shapes=[
            flat, flat, flat, taps, flat,
            pltpu.VMEM(out_weight.shape, bf16),
            turned, turned, turned, turned, turned_f32, turned_f32,
            by_chip, by_chip, by_chip, by_chip,
            pltpu.VMEM((n_wid, length, width), bf16),
            pltpu.VMEM((length, width), f32),
            turned, turned,
            flat, flat, flat, flat,
            taps, taps,
            pltpu.VMEM((n_tok, groups // owners, kernel_size), f32),
            taps,
            dma((5,)), dma((5,)), dma((n_wid * pieces,)),
            dma((pieces,)), dma((pieces,)),
            dma((chips * pieces,)), dma((chips * pieces,)), dma((chips * pieces,)), dma((chips * pieces,)),
            dma((pieces,)), dma((pieces,)),
            dma((chips * pieces,)), dma((chips * pieces,)), dma((chips * pieces,)), dma((chips * pieces,)),
            dma((pieces,)), dma((pieces,)),
            dma((n_tok,)), dma((n_tok,)), dma((n_tok,)), dma((n_tok,)),
        ],
        compiler_params=pltpu.CompilerParams(
            collective_id=0, has_side_effects=True, vmem_limit_bytes=60 * 2**20
        ),
        cost_estimate=pl.CostEstimate(
            flops=4 * length * width * width * n_wid, bytes_accessed=2 * width * width * n_wid, transcendentals=0
        ),
    )(queries, key_branch, value_branch, filters, out_weight, cotangent)
    return pl.pallas_call(
        hand_on, in_specs=[hbm] * 5, out_specs=[hbm] * 5, out_shape=results, scratch_shapes=[flat] * 4 + [taps, dma((5,)), dma((5,))]
    )(*outs)


def solution(mesh):
    return jax.shard_map(
        local,
        mesh=mesh,
        in_specs=(
            P("tok", "wid"),
            P("tok", "wid"),
            P("tok", "wid"),
            P("wid", None),
            P(None, "wid"),
            P("tok", "wid"),
        ),
        out_specs=(
            P("tok", "wid"),
            P("tok", "wid"),
            P("tok", "wid"),
            P("tok", "wid"),
            P("wid", None),
        ),
        check_vma=False,
    )
```
